32 devices in a mesh: groups: 2 (over x), fsdp: 8 (over z, y), seq: 2 (over core).
Axes of the slice: x: 2, y: 2, z: 4, core: 2. Of those that a mesh axis runs over, the one named last changes fastest.
Arguments:
- frames: bfloat16 [16, 768, 3072], P(('groups', 'fsdp'), 'seq'), parts along dimension 0, may hold values from -6 to 6
- frozen_query_key_value: bfloat16 [3, 3072, 1536], P(None, 'fsdp', 'seq'), may hold values from -0.109375 to 0.109375
- adapter_down_weight: bfloat16 [3, 3072, 64], P(None, 'fsdp'), may hold values from -0.109375 to 0.109375
- adapter_up_weight: bfloat16 [3, 64, 1536], P(None, None, 'seq'), may hold values from -0.75 to 0.75
- query_key_norm_gain: float32 [2, 1536], P(None, 'seq'), may hold values from 0.5 to 6
Outputs:
- attended: bfloat16 [16, 768, 1536], P(('groups', 'fsdp'), 'seq'), parts along dimension 0
The draws below stay inside these ranges and needn't reach their ends.
There are 2 independent parts, one for each index of `groups`. The reference program is written for one: setup_inputs(seed, part) draws one part's arguments, and reference() takes and returns one part's arrays. A program takes and returns all parts, laid end to end along the dimension named above; an argument that names none is the same for every part. Nothing has to cross between parts.
All inputs are finite; a program needn't handle non-finite values.
Results may differ from the reference program's by a relative error of at most 0.0085.
The reference program's roundings to bfloat16 on the way count: a program that leaves them out, or rounds other values in their place, can miss the bound.
Values may be sent and summed in bfloat16 or wider, within the bound.
A program may use at most 64 MiB of HBM per device.

```python
import math
import jax
import jax.numpy as jnp
from jax import lax

MODEL_WIDTH = 3072
HEAD = 128
ADAPTER_RANK = 64
HEAD_FEATURES = 1536
TOKENS = 768
CLIPS = 8


def draw_query_key_norm_gain(key, part):
    key = jax.random.fold_in(key, 11)
    low, high = (math.log(0.6), math.log(1.8))
    spread = jax.random.uniform(key, (2, HEAD_FEATURES), jnp.float32, minval=low, maxval=high)
    return jnp.exp(spread)


def shard_levels(own_key, extent, pieces, smallest, high):
    factor_of, own = 1.0, jax.random.fold_in(own_key, 6)
    for axis_at, parts in pieces:
        steps = jnp.exp(jax.random.uniform(jax.random.fold_in(own, axis_at), (parts,), jnp.float32, smallest / len(pieces), high / len(pieces)))
        factor_of = factor_of * jnp.repeat(steps, extent[axis_at] // parts).reshape([-1 if axis == axis_at else 1 for axis in range(len(extent))])
    return factor_of


def scatter_about(rng, shape, deviation, most, shards=(), kind=jnp.bfloat16):
    result = jax.random.normal(rng, shape, jnp.float32) * deviation
    if len(shards) > 0:
        result = shard_levels(rng, shape, shards, -0.22, 0.18) * result
    return jnp.clip(result, min=-most, max=most).astype(kind)


def setup_inputs(seed: int = 0, part: int = 0) -> dict:
    arg_keys = jax.random.split(jax.random.key(seed), 6)
    own_keys = jax.random.split(jax.random.fold_in(arg_keys[5], part), 6)
    frames = scatter_about(own_keys[0], (CLIPS, TOKENS, MODEL_WIDTH), 1.0, 6.0, ((0, 8), (1, 2)))
    frozen_query_key_value = scatter_about(arg_keys[1], (3, MODEL_WIDTH, HEAD_FEATURES), MODEL_WIDTH ** -0.5, 0.109375, ((1, 8), (2, 2)))
    adapter_down_weight = scatter_about(arg_keys[2], (3, MODEL_WIDTH, ADAPTER_RANK), MODEL_WIDTH ** -0.5, 0.109375, ((1, 8),))
    adapter_up_weight = scatter_about(arg_keys[3], (3, ADAPTER_RANK, HEAD_FEATURES), ADAPTER_RANK ** -0.5, 0.75, ((2, 2),))
    query_key_norm_gain = draw_query_key_norm_gain(jax.random.fold_in(arg_keys[5], 71), part)
    return dict(frames=frames, frozen_query_key_value=frozen_query_key_value, adapter_down_weight=adapter_down_weight, adapter_up_weight=adapter_up_weight, query_key_norm_gain=query_key_norm_gain)


def head_norm(block, gain_rows):
    scale = lax.rsqrt(lax.optimization_barrier(jnp.mean(block * block, axis=-1, keepdims=True)) + 1e-06)
    return (block * scale * gain_rows).astype(jnp.bfloat16)

def attend(mixed, query_key_norm_gain):
    tokens = mixed.shape[1]
    heads_here = mixed.shape[2] // HEAD
    split_heads = mixed.reshape(3, tokens, heads_here, HEAD)
    gains = query_key_norm_gain.reshape(2, heads_here, HEAD)
    queries = head_norm(split_heads[0], gains[0])
    key_rows = head_norm(split_heads[1], gains[1])
    values = split_heads[2].astype(jnp.bfloat16)
    scores = jnp.einsum('thd,shd->hts', queries.astype(jnp.float32), key_rows.astype(jnp.float32)) / jnp.sqrt(jnp.float32(HEAD))
    probs = jax.nn.softmax(scores, axis=-1).astype(jnp.bfloat16)
    attended = jnp.einsum('hts,shd->thd', probs.astype(jnp.float32), values.astype(jnp.float32))
    return attended.astype(jnp.bfloat16).reshape(tokens, heads_here * HEAD)

def reference(frames, frozen_query_key_value, adapter_down_weight, adapter_up_weight, query_key_norm_gain):
    adapter_product = jnp.einsum('enq,eqs->ens', adapter_down_weight.astype(jnp.float32), adapter_up_weight.astype(jnp.float32))
    combined_weight = (frozen_query_key_value.astype(jnp.float32) + 0.5 * adapter_product).astype(jnp.bfloat16)
    wide = jnp.transpose(combined_weight, (1, 0, 2)).reshape(MODEL_WIDTH, 3 * HEAD_FEATURES)

    def one_clip(clip_rows):
        mixed = jnp.dot(clip_rows, wide, preferred_element_type=jnp.float32)
        mixed = jnp.transpose(mixed.reshape(TOKENS, 3, HEAD_FEATURES), (1, 0, 2))
        return attend(mixed, query_key_norm_gain)
    return lax.map(one_clip, frames)
```

```python
import functools
import math

import jax
import jax.numpy as jnp
from jax import lax
from jax.experimental import pallas as pl
from jax.experimental.pallas import tpu as pltpu
from jax.sharding import PartitionSpec as P

HEAD = 128
MESH = pl.DeviceIdType.MESH
adapter_scale = 0.5
ROW_BLOCK = 256


def line_shape(devices):
    fast = 1
    while (fast * 2) ** 2 <= devices:
        fast *= 2
    return devices // fast, fast


def kernel(
    slow, fast, heads,
    frames, frozen, down, up, gain,
    out,
    clip_buf, weight_buf, total, out_buf, key_buf, value_buf,
    weight_send, weight_recv,
    peer_send, peer_recv, sib_send, sib_recv, fwd_send, fwd_recv, own_sem,
    out_send, out_recv, out_local,
):
    x, f, c = lax.axis_index("groups"), lax.axis_index("fsdp"), lax.axis_index("seq")
    i, j = lax.div(f, fast), lax.rem(f, fast)
    rows = frozen.shape[1]
    half = frames.shape[1]
    tokens = 2 * half
    group_rows = fast * rows
    sibling, peer, cross = (x, f, 1 - c), (1 - x, f, c), (1 - x, f, 1 - c)
    steps = {
        0: ((x, f + fast, c), i + 1 < slow),
        1: ((x, f - fast, c), i > 0),
        2: ((x, f + 1, c), j + 1 < fast),
        3: ((x, f - 1, c), j > 0),
    }

    barrier = pltpu.get_barrier_semaphore()
    for device in (sibling, peer, cross):
        pl.semaphore_signal(barrier, inc=1, device_id=device, device_id_type=MESH)
    expected = jnp.int32(3)
    for device, there in steps.values():
        expected = expected + there.astype(jnp.int32)

        @pl.when(there)
        def _(device=device):
            pl.semaphore_signal(barrier, inc=1, device_id=device, device_id_type=MESH)

    def head_columns(h):
        return pl.ds(pl.multiple_of((heads * x + h) * HEAD, HEAD), HEAD)

    def merge(h):
        for p in range(3):
            product = jnp.dot(
                down[p], up[p, :, head_columns(h)], preferred_element_type=jnp.float32
            )
            merged = frozen[p, :, head_columns(h)].astype(jnp.float32) + adapter_scale * product
            weight_buf[h, pl.ds(pl.multiple_of(f * rows, rows), rows), p * HEAD:(p + 1) * HEAD] = (
                merged.astype(jnp.bfloat16)
            )

    merge(0)
    pl.semaphore_wait(barrier, expected)

    def chunk(k):
        return pl.ds(k * group_rows, group_rows)

    def buf_rows(clip, part):
        return pl.ds(pl.multiple_of(clip * tokens + part * half, half), half)

    def own_copy(k):
        return pltpu.make_async_copy(
            frames.at[0, :, chunk(k)], clip_buf.at[buf_rows(0, c), chunk(k)], own_sem.at[k]
        )

    def sib_copy(k):
        return pltpu.make_async_remote_copy(
            src_ref=frames.at[0, :, chunk(k)],
            dst_ref=clip_buf.at[buf_rows(0, c), chunk(k)],
            send_sem=sib_send.at[k], recv_sem=sib_recv.at[k],
            device_id=sibling, device_id_type=MESH,
        )

    def peer_copy(k):
        return pltpu.make_async_remote_copy(
            src_ref=frames.at[0, :, chunk(k)],
            dst_ref=clip_buf.at[buf_rows(1, c), chunk(k)],
            send_sem=peer_send.at[k], recv_sem=peer_recv.at[k],
            device_id=peer, device_id_type=MESH,
        )

    def fwd_copy(k):
        return pltpu.make_async_remote_copy(
            src_ref=clip_buf.at[buf_rows(1, c), chunk(k)],
            dst_ref=clip_buf.at[buf_rows(1, c), chunk(k)],
            send_sem=fwd_send.at[k], recv_sem=fwd_recv.at[k],
            device_id=sibling, device_id_type=MESH,
        )

    def weight_copy(way, h, shard):
        block = weight_buf.at[h, pl.ds(pl.multiple_of(shard * rows, rows), rows), :]
        return pltpu.make_async_remote_copy(
            src_ref=block, dst_ref=block,
            send_sem=weight_send.at[way, h, shard], recv_sem=weight_recv.at[h, shard],
            device_id=steps[way][0], device_id_type=MESH,
        )

    def send(ways, h, shard):
        for way in ways:
            @pl.when(steps[way][1])
            def _(way=way):
                weight_copy(way, h, shard).start()

    def arrive(h, shard):
        weight_copy(0, h, shard).wait_recv()

    def slow_step(h, d):
        @pl.when(i - d >= 0)
        def _():
            shard = (i - d) * fast + j
            arrive(h, shard)
            send((0, 2, 3), h, shard)

        @pl.when(i + d < slow)
        def _():
            shard = (i + d) * fast + j
            arrive(h, shard)
            send((1, 2, 3), h, shard)

    def fast_line(h, k):
        def body(e, carry):
            @pl.when(j - e >= 0)
            def _():
                arrive(h, k * fast + j - e)
                if fast > 2:
                    send((2,), h, k * fast + j - e)

            @pl.when(j + e < fast)
            def _():
                arrive(h, k * fast + j + e)
                if fast > 2:
                    send((3,), h, k * fast + j + e)
            return carry
        lax.fori_loop(1, fast, body, 0)

    def accumulate(h, k, first_row, row_count, fresh):
        columns = pl.ds(pl.multiple_of(k * group_rows, group_rows), group_rows)

        def body(b, carry):
            at = pl.ds(pl.multiple_of(first_row + b * ROW_BLOCK, ROW_BLOCK), ROW_BLOCK)
            product = jnp.dot(
                clip_buf[at, columns], weight_buf[h, columns, :],
                preferred_element_type=jnp.float32,
            )
            if fresh:
                total[h, at, :] = product
            else:
                total[h, at, :] += product
            return carry
        lax.fori_loop(0, row_count // ROW_BLOCK, body, 0)

    def fast_step(h, d, row_count):
        if d == 0:
            fast_line(h, i)
            accumulate(h, i, 0, row_count, True)
            return

        @pl.when(i - d >= 0)
        def _():
            fast_line(h, i - d)
            accumulate(h, i - d, 0, row_count, False)

        @pl.when(i + d < slow)
        def _():
            fast_line(h, i + d)
            accumulate(h, i + d, 0, row_count, False)

    def out_copy(way, h):
        clip = 0 if way == 0 else 1
        part = c if way == 1 else 1 - c
        device = (sibling, peer, cross)[way]
        column = ((2 * c + x) * heads + h) * HEAD
        return pltpu.make_async_remote_copy(
            src_ref=out_buf.at[clip, h, pl.ds(pl.multiple_of(part * half, half), half), :],
            dst_ref=out.at[0, :, pl.ds(pl.multiple_of(column, HEAD), HEAD)],
            send_sem=out_send.at[way, h], recv_sem=out_recv.at[way, h],
            device_id=device, device_id_type=MESH,
        )

    def out_arrived(way, h):
        source_x, source_c = ((x, 1 - c), (1 - x, c), (1 - x, 1 - c))[way]
        column = ((2 * source_c + source_x) * heads + h) * HEAD
        pltpu.make_async_remote_copy(
            src_ref=out_buf.at[0, h, pl.ds(0, half), :],
            dst_ref=out.at[0, :, pl.ds(pl.multiple_of(column, HEAD), HEAD)],
            send_sem=out_send.at[way, h], recv_sem=out_recv.at[way, h],
            device_id=(sibling, peer, cross)[way], device_id_type=MESH,
        ).wait_recv()

    def out_own(h):
        column = ((2 * c + x) * heads + h) * HEAD
        return pltpu.make_async_copy(
            out_buf.at[0, h, pl.ds(pl.multiple_of(c * half, half), half), :],
            out.at[0, :, pl.ds(pl.multiple_of(column, HEAD), HEAD)],
            out_local.at[h],
        )

    def head_norm(block, gain_row):
        scale = lax.rsqrt(jnp.mean(block * block, axis=-1, keepdims=True) + 1e-06)
        return (block * scale * gain_row).astype(jnp.bfloat16)

    exponent = math.log2(math.e) / math.sqrt(HEAD)

    def attend(clip, h):
        query_gain = gain[0:1, head_columns(h)]
        key_gain = gain[1:2, head_columns(h)]

        def prepare(b, carry):
            at = pl.ds(pl.multiple_of(b * ROW_BLOCK, ROW_BLOCK), ROW_BLOCK)
            source = pl.ds(pl.multiple_of(clip * tokens + b * ROW_BLOCK, ROW_BLOCK), ROW_BLOCK)
            key_buf[at, :] = head_norm(total[h, source, HEAD:2 * HEAD], key_gain)
            value_buf[at, :] = total[h, source, 2 * HEAD:].astype(jnp.bfloat16)
            return carry
        lax.fori_loop(0, tokens // ROW_BLOCK, prepare, 0)

        def body(b, carry):
            at = pl.ds(pl.multiple_of(b * ROW_BLOCK, ROW_BLOCK), ROW_BLOCK)
            source = pl.ds(pl.multiple_of(clip * tokens + b * ROW_BLOCK, ROW_BLOCK), ROW_BLOCK)
            queries = head_norm(total[h, source, 0:HEAD], query_gain)
            scores = lax.dot_general(
                queries, key_buf[...], (((1,), (1,)), ((), ())),
                preferred_element_type=jnp.float32,
            )
            most = jnp.max(scores, axis=-1, keepdims=True)
            weights = jnp.exp2((scores - most) * exponent)
            share = 1.0 / jnp.sum(weights, axis=-1, keepdims=True)
            probs = (weights * share).astype(jnp.bfloat16)
            out_buf[clip, h, at, :] = jnp.dot(
                probs, value_buf[...], preferred_element_type=jnp.float32
            ).astype(jnp.bfloat16)
            return carry
        lax.fori_loop(0, tokens // ROW_BLOCK, body, 0)

        if clip == 0:
            out_copy(0, h).start()
            out_own(h).start()
        else:
            out_copy(1, h).start()
            out_copy(2, h).start()

    send((0, 1, 2, 3), 0, f)
    for k in range(min(2, slow)):
        peer_copy(k).start()
    for k in range(slow):
        own_copy(k).start()
        sib_copy(k).start()
    for h in range(1, heads):
        merge(h)

    last = heads - 1
    for t in range(heads * slow + 1):
        h, d = divmod(t, slow)
        if t < heads * slow and d > 0:
            slow_step(h, d)
        if (t + 2) % slow == 0 and 1 <= (t + 2) // slow <= last:
            send((0, 1, 2, 3), (t + 2) // slow, f)
        if t >= 2 and t % 2 == 0 and (t - 2) // 2 < slow:
            k = (t - 2) // 2
            peer_copy(k).wait()
            if k + 2 < slow:
                peer_copy(k + 2).start()
            fwd_copy(k).start()
        if t == slow + 1:
            for k in range(slow):
                if 2 * k + 3 <= slow:
                    accumulate(0, k, tokens, tokens, k == 0)
        if t >= 3 and t % 2 == 1 and (t - 3) // 2 < slow:
            k = (t - 3) // 2
            fwd_copy(k).wait()
            if t > slow:
                accumulate(0, k, tokens, tokens, k == 0)
        if t == 1:
            for k in range(slow):
                own_copy(k).wait()
                sib_copy(k).wait()
        if t >= 1:
            h, d = divmod(t - 1, slow)
            fast_step(h, d, 2 * tokens if h == last else tokens)
            if d == slow - 1 and h < last:
                attend(0, h)
        if t == 2 * slow + 1:
            attend(1, 0)
        if t == 2 * slow + 2:
            for k in range(slow):
                accumulate(1, k, tokens, tokens, k == 0)
            attend(1, 1)

    attend(1, last)
    attend(0, last)

    for h in range(heads):
        def sent(shard, carry, h=h):
            k, jj = lax.div(shard, fast), lax.rem(shard, fast)
            mine = jj == j
            for way, which in (
                (0, mine & (k <= i)), (1, mine & (k >= i)), (2, jj <= j), (3, jj >= j)
            ):
                @pl.when(steps[way][1] & which)
                def _(way=way):
                    weight_copy(way, h, shard).wait_send()
            return carry
        lax.fori_loop(0, slow * fast, sent, 0)
        out_own(h).wait()
        for way in range(3):
            out_copy(way, h).wait_send()
            out_arrived(way, h)


def per_device(
    devices, frames, frozen_query_key_value, adapter_down_weight, adapter_up_weight,
    query_key_norm_gain,
):
    slow, fast = line_shape(devices)
    _, half, _ = frames.shape
    _, rows, columns = frozen_query_key_value.shape
    heads = columns // HEAD // 2
    depth = rows * devices
    wide = 3 * HEAD
    dma = pltpu.SemaphoreType.DMA
    vmem = pl.BlockSpec(memory_space=pltpu.VMEM)
    hbm = pl.BlockSpec(memory_space=pl.ANY)
    return pl.pallas_call(
        functools.partial(kernel, slow, fast, heads),
        out_shape=jax.ShapeDtypeStruct((1, half, 2 * columns), jnp.bfloat16),
        in_specs=[hbm, vmem, vmem, vmem, vmem],
        out_specs=hbm,
        scratch_shapes=[
            pltpu.VMEM((4 * half, depth), jnp.bfloat16),
            pltpu.VMEM((heads, depth, wide), jnp.bfloat16),
            pltpu.VMEM((heads, 4 * half, wide), jnp.float32),
            pltpu.VMEM((2, heads, 2 * half, HEAD), jnp.bfloat16),
            pltpu.VMEM((2 * half, HEAD), jnp.bfloat16),
            pltpu.VMEM((2 * half, HEAD), jnp.bfloat16),
            dma((4, heads, devices)),
            dma((heads, devices)),
            dma((slow,)), dma((slow,)), dma((slow,)), dma((slow,)), dma((slow,)), dma((slow,)),
            dma((slow,)),
            dma((3, heads)), dma((3, heads)), dma((heads,)),
        ],
        compiler_params=pltpu.CompilerParams(
            collective_id=0, has_side_effects=True, vmem_limit_bytes=56 * 1024 * 1024
        ),
    )(
        frames, frozen_query_key_value, adapter_down_weight, adapter_up_weight,
        query_key_norm_gain,
    )


def solution(mesh):
    placed = (
        P(("groups", "fsdp"), "seq", None),
        P(None, "fsdp", "seq"),
        P(None, "fsdp", None),
        P(None, None, "seq"),
        P(None, "seq"),
    )
    return jax.shard_map(
        functools.partial(per_device, mesh.shape["fsdp"]),
        mesh=mesh,
        in_specs=placed,
        out_specs=P(("groups", "fsdp"), "seq", None),
        check_vma=False,
    )
```

```python
import functools
import math

import jax
import jax.numpy as jnp
from jax import lax
from jax.experimental import pallas as pl
from jax.experimental.pallas import tpu as pltpu
from jax.sharding import PartitionSpec as P

HEAD = 128
MESH = pl.DeviceIdType.MESH
adapter_scale = 0.5
ROW_BLOCK = 256
PARTS = 2


def line_shape(devices):
    fast = 1
    while (fast * 2) ** 2 <= devices:
        fast *= 2
    return devices // fast, fast


def kernel(
    slow, fast, heads,
    frames, frozen, down, up, gain,
    out,
    clip_buf, weight_buf, total, out_buf, key_buf, value_buf, frozen_buf,
    weight_send, weight_recv, side_send, side_recv, frozen_sem,
    peer_send, peer_recv, sib_send, sib_recv, fwd_send, fwd_recv, own_sem,
    out_send, out_recv, out_local,
):
    x, f, c = lax.axis_index("groups"), lax.axis_index("fsdp"), lax.axis_index("seq")
    i, j = lax.div(f, fast), lax.rem(f, fast)
    rows = frozen.shape[1]
    half = frames.shape[1]
    tokens = 2 * half
    group_rows = fast * rows
    side_rows = max(16, rows // 96 * 16)
    sibling, peer, cross = (x, f, 1 - c), (1 - x, f, c), (1 - x, f, 1 - c)
    steps = {
        0: ((x, f + fast, c), i + 1 < slow),
        1: ((x, f - fast, c), i > 0),
        2: ((x, f + 1, c), j + 1 < fast),
        3: ((x, f - 1, c), j > 0),
    }

    own_heads = pltpu.make_async_copy(
        frozen.at[:, :, pl.ds(pl.multiple_of(heads * x * HEAD, HEAD), heads * HEAD)],
        frozen_buf, frozen_sem,
    )
    own_heads.start()

    barrier = pltpu.get_barrier_semaphore()
    for device in (sibling, peer, cross):
        pl.semaphore_signal(barrier, inc=1, device_id=device, device_id_type=MESH)
    expected = jnp.int32(3)
    for device, there in steps.values():
        expected = expected + there.astype(jnp.int32)

        @pl.when(there)
        def _(device=device):
            pl.semaphore_signal(barrier, inc=1, device_id=device, device_id_type=MESH)

    def head_columns(h):
        return pl.ds(pl.multiple_of((heads * x + h) * HEAD, HEAD), HEAD)

    def merge(h):
        for p in range(3):
            product = lax.dot_general(
                down[p], up[p, :, head_columns(h)], (((0,), (0,)), ((), ())),
                preferred_element_type=jnp.float32,
            )
            merged = (
                frozen_buf[p, :, h * HEAD:(h + 1) * HEAD].astype(jnp.float32)
                + adapter_scale * product
            )
            weight_buf[h, pl.ds(pl.multiple_of(f * rows, rows), rows), p * HEAD:(p + 1) * HEAD] = (
                merged.astype(jnp.bfloat16)
            )

    pl.semaphore_wait(barrier, expected)

    def chunk(k):
        return pl.ds(k * group_rows, group_rows)

    def buf_rows(clip, part):
        return pl.ds(pl.multiple_of(clip * tokens + part * half, half), half)

    def own_copy(k):
        return pltpu.make_async_copy(
            frames.at[0, :, chunk(k)], clip_buf.at[buf_rows(0, c), chunk(k)], own_sem.at[k]
        )

    def sib_copy(k):
        return pltpu.make_async_remote_copy(
            src_ref=frames.at[0, :, chunk(k)],
            dst_ref=clip_buf.at[buf_rows(0, c), chunk(k)],
            send_sem=sib_send.at[k], recv_sem=sib_recv.at[k],
            device_id=sibling, device_id_type=MESH,
        )

    def peer_copy(k):
        return pltpu.make_async_remote_copy(
            src_ref=frames.at[0, :, chunk(k)],
            dst_ref=clip_buf.at[buf_rows(1, c), chunk(k)],
            send_sem=peer_send.at[k], recv_sem=peer_recv.at[k],
            device_id=peer, device_id_type=MESH,
        )

    def fwd_copy(k):
        return pltpu.make_async_remote_copy(
            src_ref=clip_buf.at[buf_rows(1, c), chunk(k)],
            dst_ref=clip_buf.at[buf_rows(1, c), chunk(k)],
            send_sem=fwd_send.at[k], recv_sem=fwd_recv.at[k],
            device_id=sibling, device_id_type=MESH,
        )

    def weight_copy(way, h, shard, main=False):
        first, count = (side_rows, rows - side_rows) if main else (0, rows)
        block = weight_buf.at[h, pl.ds(pl.multiple_of(shard * rows + first, 16), count), :]
        return pltpu.make_async_remote_copy(
            src_ref=block, dst_ref=block,
            send_sem=weight_send.at[way, h, shard], recv_sem=weight_recv.at[h, shard],
            device_id=steps[way][0], device_id_type=MESH,
        )

    def side_copy(way, h, shard):
        block = weight_buf.at[h, pl.ds(pl.multiple_of(shard * rows, 16), side_rows), :]
        return pltpu.make_async_remote_copy(
            src_ref=block, dst_ref=block,
            send_sem=side_send.at[way, h, shard], recv_sem=side_recv.at[h, shard],
            device_id=steps[way][0], device_id_type=MESH,
        )

    def send(ways, h, shard, main=False):
        for way in ways:
            @pl.when(steps[way][1])
            def _(way=way):
                weight_copy(way, h, shard, main).start()

    def send_side(ways, h, shard):
        for way in ways:
            @pl.when(steps[way][1])
            def _(way=way):
                side_copy(way, h, shard).start()

    def arrive(h, shard, main=False):
        weight_copy(0, h, shard, main).wait_recv()

    def slow_step(h, d):
        @pl.when(i - d >= 0)
        def _():
            shard = (i - d) * fast + j
            arrive(h, shard)
            send((0,), h, shard)
            send((2, 3), h, shard, True)

        @pl.when(i + d < slow)
        def _():
            shard = (i + d) * fast + j
            arrive(h, shard)
            send((1,), h, shard)
            send((2, 3), h, shard, True)

    def fast_line(h, k, ways):
        own = len(ways) == 2

        def body(e, carry):
            for jj, there, way in ((j - e, j - e >= 0, 2), (j + e, j + e < fast, 3)):
                @pl.when(there)
                def _(jj=jj, way=way):
                    shard = k * fast + jj
                    arrive(h, shard, not own)
                    if fast > 2:
                        send((way,), h, shard, not own)
                    if not own:
                        side_copy(0, h, shard).wait_recv()
                    send_side(ways, h, shard)
            return carry
        lax.fori_loop(1, fast, body, 0)

    def accumulate(h, k, first_row, row_count, fresh):
        columns = pl.ds(pl.multiple_of(k * group_rows, group_rows), group_rows)

        def body(b, carry):
            at = pl.ds(pl.multiple_of(first_row + b * ROW_BLOCK, ROW_BLOCK), ROW_BLOCK)
            product = jnp.dot(
                clip_buf[at, columns], weight_buf[h, columns, :],
                preferred_element_type=jnp.float32,
            )
            if fresh:
                total[h, at, :] = product
            else:
                total[h, at, :] += product
            return carry
        lax.fori_loop(0, row_count // ROW_BLOCK, body, 0)

    def fast_step(h, d, row_count):
        if d == 0:
            fast_line(h, i, (0, 1))
            accumulate(h, i, 0, row_count, True)
            return

        @pl.when(i - d >= 0)
        def _():
            fast_line(h, i - d, (0,))
            accumulate(h, i - d, 0, row_count, False)

        @pl.when(i + d < slow)
        def _():
            fast_line(h, i + d, (1,))
            accumulate(h, i + d, 0, row_count, False)

    def out_copy(way, h):
        clip = 0 if way == 0 else 1
        part = c if way == 1 else 1 - c
        device = (sibling, peer, cross)[way]
        column = ((2 * c + x) * heads + h) * HEAD
        return pltpu.make_async_remote_copy(
            src_ref=out_buf.at[clip, h, pl.ds(pl.multiple_of(part * half, half), half), :],
            dst_ref=out.at[0, :, pl.ds(pl.multiple_of(column, HEAD), HEAD)],
            send_sem=out_send.at[way, h], recv_sem=out_recv.at[way, h],
            device_id=device, device_id_type=MESH,
        )

    def out_arrived(way, h):
        source_x, source_c = ((x, 1 - c), (1 - x, c), (1 - x, 1 - c))[way]
        column = ((2 * source_c + source_x) * heads + h) * HEAD
        pltpu.make_async_remote_copy(
            src_ref=out_buf.at[0, h, pl.ds(0, half), :],
            dst_ref=out.at[0, :, pl.ds(pl.multiple_of(column, HEAD), HEAD)],
            send_sem=out_send.at[way, h], recv_sem=out_recv.at[way, h],
            device_id=(sibling, peer, cross)[way], device_id_type=MESH,
        ).wait_recv()

    def out_own(h):
        column = ((2 * c + x) * heads + h) * HEAD
        return pltpu.make_async_copy(
            out_buf.at[0, h, pl.ds(pl.multiple_of(c * half, half), half), :],
            out.at[0, :, pl.ds(pl.multiple_of(column, HEAD), HEAD)],
            out_local.at[h],
        )

    def head_norm(block, gain_row):
        scale = lax.rsqrt(jnp.mean(block * block, axis=-1, keepdims=True) + 1e-06)
        return (block * scale * gain_row).astype(jnp.bfloat16)

    exponent = math.log2(math.e) / math.sqrt(HEAD)

    def attend(clip, h):
        query_gain = gain[0:1, head_columns(h)]
        key_gain = gain[1:2, head_columns(h)]

        def prepare(b, carry):
            at = pl.ds(pl.multiple_of(b * ROW_BLOCK, ROW_BLOCK), ROW_BLOCK)
            source = pl.ds(pl.multiple_of(clip * tokens + b * ROW_BLOCK, ROW_BLOCK), ROW_BLOCK)
            key_buf[at, :] = head_norm(total[h, source, HEAD:2 * HEAD], key_gain)
            value_buf[at, :] = total[h, source, 2 * HEAD:].astype(jnp.bfloat16)
            return carry
        lax.fori_loop(0, tokens // ROW_BLOCK, prepare, 0)

        for part in (1 - c, c):
            for b in range(PARTS):
                size = half // PARTS
                at = pl.ds(pl.multiple_of(part * half + b * size, size), size)
                source = pl.ds(pl.multiple_of(clip * tokens + part * half + b * size, size), size)
                queries = head_norm(total[h, source, 0:HEAD], query_gain)
                scores = lax.dot_general(
                    queries, key_buf[...], (((1,), (1,)), ((), ())),
                    preferred_element_type=jnp.float32,
                )
                most = jnp.max(scores, axis=-1, keepdims=True)
                weights = jnp.exp2((scores - most) * exponent)
                share = 1.0 / jnp.sum(weights, axis=-1, keepdims=True)
                probs = (weights * share).astype(jnp.bfloat16)
                out_buf[clip, h, at, :] = jnp.dot(
                    probs, value_buf[...], preferred_element_type=jnp.float32
                ).astype(jnp.bfloat16)
            if clip == 1:
                out_copy(1 if part is c else 2, h).start()
            elif part is c:
                out_own(h).start()
            else:
                out_copy(0, h).start()

    for k in range(min(2, slow)):
        peer_copy(k).start()
    own_heads.wait()
    merge(0)
    send((0, 1, 2, 3), 0, f)
    for k in range(slow):
        own_copy(k).start()
        sib_copy(k).start()
    for h in range(1, heads):
        merge(h)

    last = heads - 1
    for t in range(heads * slow + 1):
        h, d = divmod(t, slow)
        if t < heads * slow and d > 0:
            slow_step(h, d)
        if t % slow == 1 and t // slow < last:
            send((0, 1, 2, 3), t // slow + 1, f)
        if t >= 2 and t % 2 == 0 and (t - 2) // 2 < slow:
            k = (t - 2) // 2
            peer_copy(k).wait()
            if k + 2 < slow:
                peer_copy(k + 2).start()
            fwd_copy(k).start()
        if t == slow + 1:
            for k in range(slow):
                if 2 * k + 3 <= slow:
                    accumulate(0, k, tokens, tokens, k == 0)
        if t >= 3 and t % 2 == 1 and (t - 3) // 2 < slow:
            k = (t - 3) // 2
            fwd_copy(k).wait()
            if t > slow:
                accumulate(0, k, tokens, tokens, k == 0)
        if t == 1:
            for k in range(slow):
                own_copy(k).wait()
                sib_copy(k).wait()
        if t >= 1:
            h, d = divmod(t - 1, slow)
            fast_step(h, d, 2 * tokens if h == last else tokens)
            if d == slow - 1 and h < last:
                attend(0, h)
        if t == 2 * slow + 1:
            attend(1, 0)
        if t == 2 * slow + 2:
            for k in range(slow):
                accumulate(1, k, tokens, tokens, k == 0)
            attend(1, 1)

    attend(1, last)
    attend(0, last)

    for h in range(heads):
        def sent(shard, carry, h=h):
            k, jj = lax.div(shard, fast), lax.rem(shard, fast)
            for way, passes in ((0, k <= i), (1, k >= i)):
                @pl.when(steps[way][1] & passes & (jj == j))
                def _(way=way):
                    weight_copy(way, h, shard).wait_send()

                @pl.when(steps[way][1] & passes & (jj != j))
                def _(way=way):
                    side_copy(way, h, shard).wait_send()
            for way, passes in ((2, jj <= j), (3, jj >= j)):
                @pl.when(steps[way][1] & passes & (k == i))
                def _(way=way):
                    weight_copy(way, h, shard).wait_send()

                @pl.when(steps[way][1] & passes & (k != i))
                def _(way=way):
                    weight_copy(way, h, shard, True).wait_send()
            return carry
        lax.fori_loop(0, slow * fast, sent, 0)
        out_own(h).wait()
        for way in range(3):
            out_copy(way, h).wait_send()
            out_arrived(way, h)


def per_device(
    devices, frames, frozen_query_key_value, adapter_down_weight, adapter_up_weight,
    query_key_norm_gain,
):
    slow, fast = line_shape(devices)
    _, half, _ = frames.shape
    _, rows, columns = frozen_query_key_value.shape
    heads = columns // HEAD // 2
    depth = rows * devices
    wide = 3 * HEAD
    dma = pltpu.SemaphoreType.DMA
    vmem = pl.BlockSpec(memory_space=pltpu.VMEM)
    hbm = pl.BlockSpec(memory_space=pl.ANY)
    return pl.pallas_call(
        functools.partial(kernel, slow, fast, heads),
        out_shape=jax.ShapeDtypeStruct((1, half, 2 * columns), jnp.bfloat16),
        in_specs=[hbm, hbm, vmem, vmem, vmem],
        out_specs=hbm,
        scratch_shapes=[
            pltpu.VMEM((4 * half, depth), jnp.bfloat16),
            pltpu.VMEM((heads, depth, wide), jnp.bfloat16),
            pltpu.VMEM((heads, 4 * half, wide), jnp.float32),
            pltpu.VMEM((2, heads, 2 * half, HEAD), jnp.bfloat16),
            pltpu.VMEM((2 * half, HEAD), jnp.bfloat16),
            pltpu.VMEM((2 * half, HEAD), jnp.bfloat16),
            pltpu.VMEM((3, rows, heads * HEAD), jnp.bfloat16),
            dma((4, heads, devices)),
            dma((heads, devices)),
            dma((2, heads, devices)),
            dma((heads, devices)),
            dma,
            dma((slow,)), dma((slow,)), dma((slow,)), dma((slow,)), dma((slow,)), dma((slow,)),
            dma((slow,)),
            dma((3, heads)), dma((3, heads)), dma((heads,)),
        ],
        compiler_params=pltpu.CompilerParams(
            collective_id=0, has_side_effects=True, vmem_limit_bytes=56 * 1024 * 1024
        ),
    )(
        frames, frozen_query_key_value, jnp.swapaxes(adapter_down_weight, 1, 2),
        adapter_up_weight, query_key_norm_gain,
    )


def solution(mesh):
    placed = (
        P(("groups", "fsdp"), "seq", None),
        P(None, "fsdp", "seq"),
        P(None, "fsdp", None),
        P(None, None, "seq"),
        P(None, "seq"),
    )
    return jax.shard_map(
        functools.partial(per_device, mesh.shape["fsdp"]),
        mesh=mesh,
        in_specs=placed,
        out_specs=P(("groups", "fsdp"), "seq", None),
        check_vma=False,
    )
```
